32 devices in a mesh: row: 4 (over y, x), col: 2 (over core), depth: 4 (over z).
Axes of the slice: x: 2, y: 2, z: 4, core: 2. Of those that a mesh axis runs over, the one named last changes fastest.
Arguments:
- blocks: bfloat16 [64, 16, 128, 128], P(('row', 'col'), 'depth'), may hold values from -2 to 2
- block_cols: int32 [64, 16], replicated, may hold values from 0 to 63, as said below
- product_cols: int32 [64, 24], P(('row', 'col')), may hold values from 0 to 63, as said below
Outputs:
- purified: bfloat16 [64, 24, 128, 128], P(('row', 'col'), 'depth')
The draws below stay inside these ranges and needn't reach their ends.
Inputs may be any that keep to these rules, and one draw needn't show every extreme that they name: `block_cols`: the 16 entries of a block row i are distinct, each within 8 of i counted cyclically modulo 64. `product_cols`: the 24 entries of a block row i are distinct, each within 16 of i counted cyclically modulo 64.
All inputs are finite; a program needn't handle non-finite values.
Results may differ from the reference program's by a relative error of at most 0.015.
Values may be sent and summed in bfloat16 or wider, within the bound.
No kernel may reach another device: no remote copies, remote signals or barrier semaphores. Data moves between devices by JAX's collectives and lax.ppermute only.
A program may use at most 128 MiB of HBM per device.

```python
import jax
import jax.numpy as jnp
from jax import lax

B = 128
RD = 8
F = 16
G = 24
NB = 64
N_DEPTH = 4


def band_pattern(key, amount, radius, extent):
    row_ids = jnp.arange(extent, dtype=jnp.int32)
    subkeys = jax.random.split(key, extent)
    shuffled = jax.vmap(lambda sub_key: jax.random.permutation(sub_key, 2 * radius + 1))(subkeys)
    chosen = shuffled[:, :amount].astype(jnp.int32)
    return ((row_ids[:, None] + chosen - radius) % extent).astype(jnp.int32)


def draw_block_cols(key, part):
    return band_pattern(jax.random.fold_in(key, 11), F, RD, NB)


def draw_product_cols(key, part):
    return band_pattern(jax.random.fold_in(key, 29), G, 2 * RD, NB)


def block_levels(key, shape, shards, low, high):
    def one(dim, parts):
        heights = jax.random.uniform(jax.random.fold_in(jax.random.fold_in(key, 6), dim), (parts,), jnp.float32, low / len(shards), high / len(shards))
        return jnp.repeat(jnp.exp(heights), shape[dim] // parts).reshape((-1,) + (1,) * (len(shape) - dim - 1))

    factor_of = one(*shards[0])
    for cut in shards[1:]:
        factor_of = factor_of * one(*cut)
    return factor_of


def scatter_about(key, shape, deviation, reach, cuts=(), kind=jnp.bfloat16):
    result = jax.random.normal(key, shape, jnp.float32) * deviation
    if len(cuts) > 0:
        result = block_levels(key, shape, cuts, -0.22, 0.18) * result
    return jnp.clip(result, min=-reach, max=reach).astype(kind)


def setup_inputs(seed: int = 0) -> dict:
    streams_of = jax.random.split(jax.random.key(seed), 4)
    blocks = scatter_about(streams_of[0], (NB, F, B, B), 0.15, 2.0, ((0, 8), (1, 4)))
    block_cols = draw_block_cols(jax.random.fold_in(streams_of[3], 71), 0)
    product_cols = draw_product_cols(jax.random.fold_in(streams_of[3], 71), 0)
    return dict(blocks=blocks, block_cols=block_cols, product_cols=product_cols)


def select_blocks(blocks, block_cols, inner_rows, targets):
    cols_of = block_cols[inner_rows]
    matches = cols_of[:, :, None] == targets[None, None, :]
    has_match = jnp.any(matches, axis=1)
    slot_ids = jnp.arange(F, dtype=jnp.int32)[None, :, None]
    position = jnp.sum(jnp.where(matches, slot_ids, 0), axis=1).astype(jnp.int32)
    picked = blocks[inner_rows[:, None], position].astype(jnp.float32)
    return jnp.where(has_match[:, :, None, None], picked, jnp.zeros((), jnp.float32))


def depth_partials(left_blocks, right_blocks, groups):
    left_group = left_blocks.reshape(groups, -1, B, B)
    right_group = right_blocks.reshape(groups, -1, right_blocks.shape[1], B, B)
    partial_value = jnp.einsum('dsab,dstbc->dtac', left_group, right_group)
    rounded = lax.optimization_barrier(partial_value.astype(jnp.bfloat16))
    return jnp.sum(rounded.astype(jnp.float32), axis=0)


def reference(blocks, block_cols, product_cols):
    def one_row(row_id):
        left_blocks = blocks[row_id].astype(jnp.float32)
        inner_rows = block_cols[row_id]
        targets = product_cols[row_id]
        right_first = select_blocks(blocks, block_cols, inner_rows, targets)
        square = depth_partials(left_blocks, right_first, N_DEPTH).astype(jnp.bfloat16)
        right_second = select_blocks(blocks, block_cols, targets, targets)
        cubed = depth_partials(square.astype(jnp.float32), right_second, N_DEPTH)
        return (3.0 * square.astype(jnp.float32) - 2.0 * cubed).astype(jnp.bfloat16)

    return lax.map(one_row, jnp.arange(NB, dtype=jnp.int32))
```

```python
import jax
import jax.numpy as jnp
from jax import lax
from jax.experimental import pallas as pl
from jax.experimental.pallas import tpu as pltpu
from jax.sharding import PartitionSpec as P

REACH = 8
WIDE = 2 * REACH
SPAN = 2 * REACH + 2


def permuted(value, axes, pairs):
    return lax.ppermute(value, axes, pairs)


def depth_pieces(own):
    count = lax.axis_size("depth")
    me = lax.axis_index("depth")
    if count != 4:
        pieces, owners = [own], [me]
        for step in range(1, count):
            pairs = [(i, (i + step) % count) for i in range(count)]
            pieces.append(permuted(own, "depth", pairs))
            owners.append((me - step) % count)
        return pieces, owners
    partner = permuted(own, "depth", [(0, 1), (1, 0), (2, 3), (3, 2)])
    across = permuted(own, "depth", [(1, 2), (2, 1)])
    across_outer = permuted(partner, "depth", [(1, 2), (2, 1)])
    outward = permuted(across, "depth", [(1, 0), (2, 3)])
    outward_outer = permuted(across_outer, "depth", [(1, 0), (2, 3)])
    at_end = jnp.logical_or(me == 0, me == 3)
    third = jnp.where(at_end, outward, across)
    fourth = jnp.where(at_end, outward_outer, across_outer)
    low = me < 2
    owners = [me, me ^ 1, jnp.where(low, 2, 1), jnp.where(low, 3, 0)]
    return [own, partner, third, fourth], owners


def row_groups(pieces):
    rows, cols = lax.axis_size("row"), lax.axis_size("col")
    axes = ("row", "col")
    if rows == 4 and cols == 2:
        place = lax.axis_index("row")
        core = lax.axis_index("col")
        even = place % 2 == 0
        swap_x = [(0, 1), (1, 0), (2, 3), (3, 2)]
        swap_y = [(0, 2), (2, 0), (1, 3), (3, 1)]
        swap_core = [(0, 1), (1, 0)]
        by_x = [permuted(p, "row", swap_x) for p in pieces]
        by_y = [permuted(p, "row", swap_y) for p in by_x]
        send_x = (core == 0) == even
        shared = [jnp.where(send_x, a, b) for a, b in zip(by_x, by_y)]
        other = [permuted(p, "col", swap_core) for p in pieces]
        shared = [permuted(p, "col", swap_core) for p in shared]
        beside = jnp.where(core == 0, 1, -1)
        over = jnp.where(even, 2, -2)
        return [pieces, other, by_x, by_y, shared], [0, beside, over, -over, -beside]
    count = rows * cols
    groups, offsets = [pieces], [0]
    for offset in (1, -1, 2, -2):
        pairs = [(i, (i - offset) % count) for i in range(count)]
        groups.append([permuted(p, axes, pairs) for p in pieces])
        offsets.append(offset)
    return groups, offsets


def purify_kernel(piece_count, piece_rows, piece_slots, own_rows, out_slots, *refs):
    place_ref, hole_ref, keep_ref, target_ref = refs[:4]
    piece_refs = refs[4 : 4 + piece_count]
    out_ref, panel, square, sem = refs[4 + piece_count :]
    window = own_rows + 2 * WIDE
    pairs = window // 2
    edge = out_ref.shape[-1]
    per_piece = piece_rows * piece_slots

    zero = jnp.zeros((edge, edge), jnp.bfloat16)

    for pair in range(pairs):
        base = pair * 2 * SPAN
        for half in range(2):
            for u in range(SPAN):
                row = 2 * pair - REACH + u
                inside = 0 <= row < window
                banded = (u < SPAN - 1) if half == 0 else (u > 0)
                if not (inside and banded):
                    panel[base + half * SPAN + u] = zero

    @pl.loop(0, window)
    def _(row):
        spot = hole_ref[row]

        @pl.when(spot >= 0)
        def _():
            panel[spot] = zero

    started = jnp.int32(0)
    for number, piece in enumerate(piece_refs):

        def start(row, done, number=number, piece=piece):
            for slot in range(piece_slots):
                spot = place_ref[number * per_piece + row * piece_slots + slot]

                @pl.when(spot >= 0)
                def _():
                    pltpu.make_async_copy(piece.at[row, slot], panel.at[spot], sem).start()

                done = done + jnp.where(spot >= 0, 1, 0)
            return done

        started = lax.fori_loop(0, piece_rows, start, started)

    @pl.loop(0, square.shape[0])
    def _(spot):
        square[spot] = zero

    @pl.loop(0, started)
    def _(_):
        pltpu.make_async_copy(piece_refs[0].at[0, 0], panel.at[0], sem).wait()

    cols = window + 2 * REACH
    first_pair = WIDE // 2

    @pl.loop(0, own_rows // 2)
    def _(pair_of_rows):
        base = (pair_of_rows + first_pair) * 2 * SPAN
        for delta in range(-REACH, REACH + 1):
            inner = range(max(delta, 0) - REACH // 2, min(delta, 0) + REACH // 2 + 1)
            left = jnp.concatenate(
                [
                    jnp.concatenate(
                        [
                            panel[base + e * 2 * SPAN + h * SPAN + a - 2 * e + REACH]
                            for e in inner
                            for h in range(2)
                        ],
                        axis=1,
                    )
                    for a in range(2)
                ],
                axis=0,
            )
            right = jnp.concatenate(
                [
                    panel[
                        pl.ds(
                            base + delta * 2 * SPAN + h * SPAN + 2 * (inner[0] - delta) + REACH,
                            2 * len(inner),
                        )
                    ].reshape(2 * len(inner) * edge, edge)
                    for h in range(2)
                ],
                axis=1,
            )
            both = jnp.dot(left, right, preferred_element_type=jnp.float32)
            for a in range(2):
                for h in range(2):
                    row = 2 * pair_of_rows + a
                    col = 2 * (pair_of_rows + first_pair + delta) + h
                    keep = keep_ref[row * window + col]
                    part = both[a * edge : (a + 1) * edge, h * edge : (h + 1) * edge]
                    part = jnp.where(keep > 0, part, 0.0)
                    square[row * cols + col + REACH] = part.astype(jnp.bfloat16)

    @pl.loop(0, own_rows)
    def _(row):
        for slot in range(out_slots):
            col = target_ref[row * out_slots + slot]
            pair = lax.shift_right_logical(col, 1)
            half = col - 2 * pair
            left = square[pl.ds(row * cols + 2 * pair, SPAN)]
            left = jnp.concatenate([left[u] for u in range(SPAN)], axis=1)
            right = panel[pl.ds((2 * pair + half) * SPAN, SPAN)].reshape(SPAN * edge, edge)
            cubed = jnp.dot(left, right, preferred_element_type=jnp.float32)
            own = square[row * cols + col + REACH].astype(jnp.float32)
            out_ref[row, slot] = (3.0 * own - 2.0 * cubed).astype(out_ref.dtype)


def local(blocks, block_cols, product_cols):
    rows, slots, edge = blocks.shape[0], blocks.shape[1], blocks.shape[2]
    order = block_cols.shape[0]
    targets = product_cols.shape[1]
    depth_count = lax.axis_size("depth")
    out_slots = targets // depth_count
    place = lax.axis_index(("row", "col"))
    depth = lax.axis_index("depth")
    window = rows + 2 * WIDE
    first = place * rows - WIDE

    pieces, owners = depth_pieces(blocks)
    groups, offsets = row_groups(pieces)

    row_ids = jnp.stack([(place + o) * rows + jnp.arange(rows) for o in offsets])
    slot_ids = jnp.stack([o * slots + jnp.arange(slots) for o in owners])
    wanted = block_cols[row_ids[:, None, :, None] % order, slot_ids[None, :, None, :]]

    def spot_of(row, col):
        pair = col // 2
        spot = (2 * pair + col % 2) * SPAN + row - 2 * pair + REACH
        return jnp.where(col < window, spot, -1).astype(jnp.int32)

    spots = spot_of(row_ids[:, None, :, None] - first, (wanted - first) % order).reshape(-1)
    all_rows = jnp.arange(window)
    filled = (block_cols[(all_rows + first) % order] - (all_rows + first)[:, None] + REACH) % order
    hole = (2 * REACH) * (2 * REACH + 1) // 2 - jnp.sum(filled, axis=1)
    hole_col = all_rows + hole - REACH
    holes = jnp.where(hole_col >= 0, spot_of(all_rows, hole_col), -1).astype(jnp.int32)
    target_cols = (product_cols - first) % order
    keep = jnp.any(target_cols[:, :, None] == jnp.arange(window), axis=1)
    mine = lax.dynamic_slice_in_dim(target_cols, depth * out_slots, out_slots, 1)

    flat = [p for group in groups for p in group]
    kernel_body = lambda *refs: purify_kernel(len(flat), rows, slots, rows, out_slots, *refs)
    smem = pl.BlockSpec(memory_space=pltpu.SMEM)
    hbm = pl.BlockSpec(memory_space=pl.ANY)
    return pl.pallas_call(
        kernel_body,
        out_shape=jax.ShapeDtypeStruct((rows, out_slots, edge, edge), jnp.bfloat16),
        in_specs=[smem] * 4 + [hbm] * len(flat),
        out_specs=pl.BlockSpec(memory_space=pltpu.VMEM),
        scratch_shapes=[
            pltpu.VMEM((window * SPAN, edge, edge), jnp.bfloat16),
            pltpu.VMEM((rows * (window + 2 * REACH), edge, edge), jnp.bfloat16),
            pltpu.SemaphoreType.DMA,
        ],
        compiler_params=pltpu.CompilerParams(vmem_limit_bytes=56 * 2**20),
        name="purify",
    )(
        spots,
        holes,
        keep.astype(jnp.int32).reshape(-1),
        mine.astype(jnp.int32).reshape(-1),
        *flat,
    )


def solution(mesh):
    placed = (P(("row", "col"), "depth", None, None), P(), P(("row", "col"), None))
    return jax.shard_map(
        local,
        mesh=mesh,
        in_specs=placed,
        out_specs=P(("row", "col"), "depth", None, None),
        check_vma=False,
    )
```

```python
import jax
import jax.numpy as jnp
from jax import lax
from jax.experimental import pallas as pl
from jax.experimental.pallas import tpu as pltpu
from jax.sharding import PartitionSpec as P

REACH = 8
WIDE = 2 * REACH
SPAN = 2 * REACH + 2


def permuted(value, axes, pairs):
    return lax.ppermute(value, axes, pairs)


together = lax.optimization_barrier


def line_window(own, extra):
    me = lax.axis_index("depth")
    core = lax.axis_index("col")
    even = lax.axis_index("row") % 2 == 0
    at_end = jnp.logical_or(me == 0, me == 3)
    ends = [(0, 1), (1, 0), (2, 3), (3, 2)]
    middle = [(1, 2), (2, 1)]
    outward = [(1, 0), (2, 3)]

    def along_x(value):
        return permuted(value, "row", [(0, 1), (1, 0), (2, 3), (3, 2)])

    def along_y(value):
        return permuted(value, "row", [(0, 2), (2, 0), (1, 3), (3, 1)])

    def over_core(value):
        return permuted(value, "col", [(0, 1), (1, 0)])

    send_x = (core == 0) == even

    def shared(by_x, by_y):
        return over_core(jnp.where(send_x, by_x, by_y))

    x0 = along_x(own)
    p1 = permuted(own, "depth", ends)
    across = permuted(own, "depth", middle)
    x0, p1, across = together((x0, p1, across))

    x1 = along_x(p1)
    y0 = along_y(x0)
    across_outer = permuted(p1, "depth", middle)
    out = permuted(across, "depth", outward)
    extra, x1, y0, across_outer, out = together((extra, x1, y0, across_outer, out))

    p2 = jnp.where(at_end, out, across)
    x2 = along_x(p2)
    y1 = along_y(x1)
    out_outer = permuted(across_outer, "depth", outward)
    c0 = over_core(own)
    s0 = shared(x0, y0)
    x2, y1, out_outer, c0, s0 = together((x2, y1, out_outer, c0, s0))

    p3 = jnp.where(at_end, out_outer, across_outer)
    x3 = along_x(p3)
    y2 = along_y(x2)
    c1 = over_core(p1)
    c2 = over_core(p2)
    s1 = shared(x1, y1)
    x3, y2, c1, c2, s1 = together((x3, y2, c1, c2, s1))

    y3 = along_y(x3)
    c3 = over_core(p3)
    s2 = shared(x2, y2)
    y3, c3, s2 = together((y3, c3, s2))
    s3 = shared(x3, y3)

    groups = [
        [own, p1, p2, p3],
        [c0, c1, c2, c3],
        [x0, x1, x2, x3],
        [y0, y1, y2, y3],
        [s0, s1, s2, s3],
    ]
    return groups, extra


def ring_window(own, extra):
    depths = lax.axis_size("depth")
    pieces = [own]
    for step in range(1, depths):
        pairs = [(i, (i + step) % depths) for i in range(depths)]
        pieces.append(permuted(own, "depth", pairs))
    count = lax.axis_size(("row", "col"))
    groups = [pieces]
    for offset in (1, -1, 2, -2):
        pairs = [(i, (i - offset) % count) for i in range(count)]
        groups.append([permuted(p, ("row", "col"), pairs) for p in pieces])
    return groups, extra


def window_plan():
    sizes = (lax.axis_size("row"), lax.axis_size("col"), lax.axis_size("depth"))
    return line_window if sizes == (4, 2, 4) else ring_window


def purify_kernel(piece_count, piece_rows, piece_slots, own_rows, out_slots, *refs):
    place_ref, hole_ref, keep_ref, target_ref = refs[:4]
    piece_refs = refs[4 : 4 + piece_count]
    out_ref, panel, square, sem = refs[4 + piece_count :]
    window = own_rows + 2 * WIDE
    pairs = window // 2
    edge = out_ref.shape[-1]
    per_piece = piece_rows * piece_slots

    zero = jnp.zeros((edge, edge), jnp.bfloat16)

    for pair in range(pairs):
        base = pair * 2 * SPAN
        for half in range(2):
            for u in range(SPAN):
                row = 2 * pair - REACH + u
                inside = 0 <= row < window
                banded = (u < SPAN - 1) if half == 0 else (u > 0)
                if not (inside and banded):
                    panel[base + half * SPAN + u] = zero

    @pl.loop(0, window)
    def _(row):
        spot = hole_ref[row]

        @pl.when(spot >= 0)
        def _():
            panel[spot] = zero

    started = jnp.int32(0)
    for number, piece in enumerate(piece_refs):

        def start(row, done, number=number, piece=piece):
            for slot in range(piece_slots):
                spot = place_ref[number * per_piece + row * piece_slots + slot]

                @pl.when(spot >= 0)
                def _():
                    pltpu.make_async_copy(piece.at[row, slot], panel.at[spot], sem).start()

                done = done + jnp.where(spot >= 0, 1, 0)
            return done

        started = lax.fori_loop(0, piece_rows, start, started)

    @pl.loop(0, square.shape[0])
    def _(spot):
        square[spot] = zero

    @pl.loop(0, started)
    def _(_):
        pltpu.make_async_copy(piece_refs[0].at[0, 0], panel.at[0], sem).wait()

    cols = window + 2 * REACH
    first_pair = WIDE // 2

    @pl.loop(0, own_rows // 2)
    def _(pair_of_rows):
        base = (pair_of_rows + first_pair) * 2 * SPAN
        for delta in range(-REACH, REACH + 1):
            inner = range(max(delta, 0) - REACH // 2, min(delta, 0) + REACH // 2 + 1)
            left = jnp.concatenate(
                [
                    jnp.concatenate(
                        [
                            panel[base + e * 2 * SPAN + h * SPAN + a - 2 * e + REACH]
                            for e in inner
                            for h in range(2)
                        ],
                        axis=1,
                    )
                    for a in range(2)
                ],
                axis=0,
            )
            right = jnp.concatenate(
                [
                    panel[
                        pl.ds(
                            base + delta * 2 * SPAN + h * SPAN + 2 * (inner[0] - delta) + REACH,
                            2 * len(inner),
                        )
                    ].reshape(2 * len(inner) * edge, edge)
                    for h in range(2)
                ],
                axis=1,
            )
            both = jnp.dot(left, right, preferred_element_type=jnp.float32)
            for a in range(2):
                for h in range(2):
                    row = 2 * pair_of_rows + a
                    col = 2 * (pair_of_rows + first_pair + delta) + h
                    keep = keep_ref[row * window + col]
                    part = both[a * edge : (a + 1) * edge, h * edge : (h + 1) * edge]
                    part = jnp.where(keep > 0, part, 0.0)
                    square[row * cols + col + REACH] = part.astype(jnp.bfloat16)

    @pl.loop(0, own_rows)
    def _(row):
        for slot in range(out_slots):
            col = target_ref[row * out_slots + slot]
            pair = lax.shift_right_logical(col, 1)
            half = col - 2 * pair
            left = square[pl.ds(row * cols + 2 * pair, SPAN)]
            left = jnp.concatenate([left[u] for u in range(SPAN)], axis=1)
            right = panel[pl.ds((2 * pair + half) * SPAN, SPAN)].reshape(SPAN * edge, edge)
            cubed = jnp.dot(left, right, preferred_element_type=jnp.float32)
            own = square[row * cols + col + REACH].astype(jnp.float32)
            out_ref[row, slot] = (3.0 * own - 2.0 * cubed).astype(out_ref.dtype)


def window_places(place, depth):
    if window_plan() is line_window:
        low = depth < 2
        owners = [depth, depth ^ 1, jnp.where(low, 2, 1), jnp.where(low, 3, 0)]
        beside = jnp.where(lax.axis_index("col") == 0, 1, -1)
        over = jnp.where(lax.axis_index("row") % 2 == 0, 2, -2)
        return owners, [0, beside, over, -over, -beside]
    depths = lax.axis_size("depth")
    return [(depth - step) % depths for step in range(depths)], [0, 1, -1, 2, -2]


def local(blocks, block_cols, product_cols):
    rows, slots, edge = blocks.shape[0], blocks.shape[1], blocks.shape[2]
    order = block_cols.shape[0]
    targets = product_cols.shape[1]
    depth_count = lax.axis_size("depth")
    out_slots = targets // depth_count
    place = lax.axis_index(("row", "col"))
    depth = lax.axis_index("depth")
    window = rows + 2 * WIDE
    first = place * rows - WIDE

    owners, offsets = window_places(place, depth)
    row_ids = jnp.stack([(place + o) * rows + jnp.arange(rows) for o in offsets])
    slot_ids = jnp.stack([o * slots + jnp.arange(slots) for o in owners])
    wanted = block_cols[row_ids[:, None, :, None] % order, slot_ids[None, :, None, :]]

    def spot_of(row, col):
        pair = col // 2
        spot = (2 * pair + col % 2) * SPAN + row - 2 * pair + REACH
        return jnp.where(col < window, spot, -1).astype(jnp.int32)

    spots = spot_of(row_ids[:, None, :, None] - first, (wanted - first) % order).reshape(-1)
    all_rows = jnp.arange(window)
    filled = (block_cols[(all_rows + first) % order] - (all_rows + first)[:, None] + REACH) % order
    hole = (2 * REACH) * (2 * REACH + 1) // 2 - jnp.sum(filled, axis=1)
    hole_col = all_rows + hole - REACH
    holes = jnp.where(hole_col >= 0, spot_of(all_rows, hole_col), -1).astype(jnp.int32)
    target_cols = (product_cols - first) % order
    keep = jnp.any(target_cols[:, :, None] == jnp.arange(window), axis=1)
    keep = keep.astype(jnp.int32).reshape(-1)
    mine = lax.dynamic_slice_in_dim(target_cols, depth * out_slots, out_slots, 1)
    mine = mine.astype(jnp.int32).reshape(-1)

    groups, tables = window_plan()(blocks, (spots, holes, keep, mine))
    flat = [p for group in groups for p in group]
    kernel_body = lambda *refs: purify_kernel(len(flat), rows, slots, rows, out_slots, *refs)
    smem = pl.BlockSpec(memory_space=pltpu.SMEM)
    hbm = pl.BlockSpec(memory_space=pl.ANY)
    return pl.pallas_call(
        kernel_body,
        out_shape=jax.ShapeDtypeStruct((rows, out_slots, edge, edge), jnp.bfloat16),
        in_specs=[smem] * 4 + [hbm] * len(flat),
        out_specs=pl.BlockSpec(memory_space=pltpu.VMEM),
        scratch_shapes=[
            pltpu.VMEM((window * SPAN, edge, edge), jnp.bfloat16),
            pltpu.VMEM((rows * (window + 2 * REACH), edge, edge), jnp.bfloat16),
            pltpu.SemaphoreType.DMA,
        ],
        compiler_params=pltpu.CompilerParams(vmem_limit_bytes=56 * 2**20),
        name="purify",
    )(*tables, *flat)


def solution(mesh):
    placed = (P(("row", "col"), "depth", None, None), P(), P(("row", "col"), None))
    return jax.shard_map(
        local,
        mesh=mesh,
        in_specs=placed,
        out_specs=P(("row", "col"), "depth", None, None),
        check_vma=False,
    )
```

```python
import jax
import jax.numpy as jnp
from jax import lax
from jax.experimental import pallas as pl
from jax.experimental.pallas import tpu as pltpu
from jax.sharding import PartitionSpec as P

REACH = 8
WIDE = 2 * REACH
SPAN = 2 * REACH + 2


def permuted(value, axes, pairs):
    return lax.ppermute(value, axes, pairs)


together = lax.optimization_barrier


def line_window(own, extra):
    send_x = (lax.axis_index("col") == 0) == (lax.axis_index("row") % 2 == 0)

    def along_z(value):
        return permuted(value, "depth", [(0, 1), (1, 2), (2, 3), (3, 0)])

    def along_x(value):
        return permuted(value, "row", [(0, 1), (1, 0), (2, 3), (3, 2)])

    def along_y(value):
        return permuted(value, "row", [(0, 2), (2, 0), (1, 3), (3, 1)])

    def over_core(value):
        return permuted(value, "col", [(0, 1), (1, 0)])

    def shared(by_x, by_y):
        return over_core(jnp.where(send_x, by_x, by_y))

    x0, p1, c0 = together((along_x(own), along_z(own), over_core(own)))
    extra, x1, y0, p2 = together((extra, along_x(p1), along_y(x0), along_z(p1)))
    x2, y1, p3, c1, s0 = together(
        (along_x(p2), along_y(x1), along_z(p2), over_core(p1), shared(x0, y0))
    )
    x3, y2, c2, c3, s1 = together(
        (along_x(p3), along_y(x2), over_core(p2), over_core(p3), shared(x1, y1))
    )
    y3, s2 = together((along_y(x3), shared(x2, y2)))
    s3 = shared(x3, y3)
    groups = [
        [own, p1, p2, p3],
        [c0, c1, c2, c3],
        [x0, x1, x2, x3],
        [y0, y1, y2, y3],
        [s0, s1, s2, s3],
    ]
    return groups, extra


def ring_window(own, extra):
    depths = lax.axis_size("depth")
    pieces = [own]
    for step in range(1, depths):
        pairs = [(i, (i + step) % depths) for i in range(depths)]
        pieces.append(permuted(own, "depth", pairs))
    count = lax.axis_size(("row", "col"))
    groups = [pieces]
    for offset in (1, -1, 2, -2):
        pairs = [(i, (i - offset) % count) for i in range(count)]
        groups.append([permuted(p, ("row", "col"), pairs) for p in pieces])
    return groups, extra


def window_plan():
    sizes = (lax.axis_size("row"), lax.axis_size("col"), lax.axis_size("depth"))
    return line_window if sizes == (4, 2, 4) else ring_window


def purify_kernel(piece_count, piece_rows, piece_slots, own_rows, out_slots, *refs):
    place_ref, hole_ref, keep_ref, target_ref = refs[:4]
    piece_refs = refs[4 : 4 + piece_count]
    out_ref, panel, square, sem = refs[4 + piece_count :]
    window = own_rows + 2 * WIDE
    pairs = window // 2
    edge = out_ref.shape[-1]
    per_piece = piece_rows * piece_slots

    zero = jnp.zeros((edge, edge), jnp.bfloat16)

    for pair in range(pairs):
        base = pair * 2 * SPAN
        for half in range(2):
            for u in range(SPAN):
                row = 2 * pair - REACH + u
                inside = 0 <= row < window
                banded = (u < SPAN - 1) if half == 0 else (u > 0)
                if not (inside and banded):
                    panel[base + half * SPAN + u] = zero

    @pl.loop(0, window)
    def _(row):
        spot = hole_ref[row]

        @pl.when(spot >= 0)
        def _():
            panel[spot] = zero

    started = jnp.int32(0)
    for number, piece in enumerate(piece_refs):

        def start(row, done, number=number, piece=piece):
            for slot in range(piece_slots):
                spot = place_ref[number * per_piece + row * piece_slots + slot]

                @pl.when(spot >= 0)
                def _():
                    pltpu.make_async_copy(piece.at[row, slot], panel.at[spot], sem).start()

                done = done + jnp.where(spot >= 0, 1, 0)
            return done

        started = lax.fori_loop(0, piece_rows, start, started)

    @pl.loop(0, square.shape[0])
    def _(spot):
        square[spot] = zero

    @pl.loop(0, started)
    def _(_):
        pltpu.make_async_copy(piece_refs[0].at[0, 0], panel.at[0], sem).wait()

    cols = window + 2 * REACH
    first_pair = WIDE // 2

    @pl.loop(0, own_rows // 2)
    def _(pair_of_rows):
        base = (pair_of_rows + first_pair) * 2 * SPAN
        for delta in range(-REACH, REACH + 1):
            inner = range(max(delta, 0) - REACH // 2, min(delta, 0) + REACH // 2 + 1)
            left = jnp.concatenate(
                [
                    jnp.concatenate(
                        [
                            panel[base + e * 2 * SPAN + h * SPAN + a - 2 * e + REACH]
                            for e in inner
                            for h in range(2)
                        ],
                        axis=1,
                    )
                    for a in range(2)
                ],
                axis=0,
            )
            right = jnp.concatenate(
                [
                    panel[
                        pl.ds(
                            base + delta * 2 * SPAN + h * SPAN + 2 * (inner[0] - delta) + REACH,
                            2 * len(inner),
                        )
                    ].reshape(2 * len(inner) * edge, edge)
                    for h in range(2)
                ],
                axis=1,
            )
            both = jnp.dot(left, right, preferred_element_type=jnp.float32)
            for a in range(2):
                for h in range(2):
                    row = 2 * pair_of_rows + a
                    col = 2 * (pair_of_rows + first_pair + delta) + h
                    keep = keep_ref[row * window + col]
                    part = both[a * edge : (a + 1) * edge, h * edge : (h + 1) * edge]
                    part = jnp.where(keep > 0, part, 0.0)
                    square[row * cols + col + REACH] = part.astype(jnp.bfloat16)

    @pl.loop(0, own_rows)
    def _(row):
        for slot in range(out_slots):
            col = target_ref[row * out_slots + slot]
            pair = lax.shift_right_logical(col, 1)
            half = col - 2 * pair
            left = square[pl.ds(row * cols + 2 * pair, SPAN)]
            left = jnp.concatenate([left[u] for u in range(SPAN)], axis=1)
            right = panel[pl.ds((2 * pair + half) * SPAN, SPAN)].reshape(SPAN * edge, edge)
            cubed = jnp.dot(left, right, preferred_element_type=jnp.float32)
            own = square[row * cols + col + REACH].astype(jnp.float32)
            out_ref[row, slot] = (3.0 * own - 2.0 * cubed).astype(out_ref.dtype)


def window_places(place, depth):
    depths = lax.axis_size("depth")
    owners = [(depth - step) % depths for step in range(depths)]
    if window_plan() is not line_window:
        return owners, [0, 1, -1, 2, -2]
    beside = jnp.where(lax.axis_index("col") == 0, 1, -1)
    over = jnp.where(lax.axis_index("row") % 2 == 0, 2, -2)
    return owners, [0, beside, over, -over, -beside]


def local(blocks, block_cols, product_cols):
    rows, slots, edge = blocks.shape[0], blocks.shape[1], blocks.shape[2]
    order = block_cols.shape[0]
    targets = product_cols.shape[1]
    depth_count = lax.axis_size("depth")
    out_slots = targets // depth_count
    place = lax.axis_index(("row", "col"))
    depth = lax.axis_index("depth")
    window = rows + 2 * WIDE
    first = place * rows - WIDE

    owners, offsets = window_places(place, depth)
    row_ids = jnp.stack([(place + o) * rows + jnp.arange(rows) for o in offsets])
    slot_ids = jnp.stack([o * slots + jnp.arange(slots) for o in owners])
    wanted = block_cols[row_ids[:, None, :, None] % order, slot_ids[None, :, None, :]]

    def spot_of(row, col):
        pair = col // 2
        spot = (2 * pair + col % 2) * SPAN + row - 2 * pair + REACH
        return jnp.where(col < window, spot, -1).astype(jnp.int32)

    spots = spot_of(row_ids[:, None, :, None] - first, (wanted - first) % order).reshape(-1)
    all_rows = jnp.arange(window)
    filled = (block_cols[(all_rows + first) % order] - (all_rows + first)[:, None] + REACH) % order
    hole = (2 * REACH) * (2 * REACH + 1) // 2 - jnp.sum(filled, axis=1)
    hole_col = all_rows + hole - REACH
    holes = jnp.where(hole_col >= 0, spot_of(all_rows, hole_col), -1).astype(jnp.int32)
    target_cols = (product_cols - first) % order
    keep = jnp.any(target_cols[:, :, None] == jnp.arange(window), axis=1)
    keep = keep.astype(jnp.int32).reshape(-1)
    mine = lax.dynamic_slice_in_dim(target_cols, depth * out_slots, out_slots, 1)
    mine = mine.astype(jnp.int32).reshape(-1)

    groups, tables = window_plan()(blocks, (spots, holes, keep, mine))
    flat = [p for group in groups for p in group]
    kernel_body = lambda *refs: purify_kernel(len(flat), rows, slots, rows, out_slots, *refs)
    smem = pl.BlockSpec(memory_space=pltpu.SMEM)
    hbm = pl.BlockSpec(memory_space=pl.ANY)
    return pl.pallas_call(
        kernel_body,
        out_shape=jax.ShapeDtypeStruct((rows, out_slots, edge, edge), jnp.bfloat16),
        in_specs=[smem] * 4 + [hbm] * len(flat),
        out_specs=pl.BlockSpec(memory_space=pltpu.VMEM),
        scratch_shapes=[
            pltpu.VMEM((window * SPAN, edge, edge), jnp.bfloat16),
            pltpu.VMEM((rows * (window + 2 * REACH), edge, edge), jnp.bfloat16),
            pltpu.SemaphoreType.DMA,
        ],
        compiler_params=pltpu.CompilerParams(vmem_limit_bytes=42 * 2**20),
        name="purify",
    )(*tables, *flat)


def solution(mesh):
    placed = (P(("row", "col"), "depth", None, None), P(), P(("row", "col"), None))
    return jax.shard_map(
        local,
        mesh=mesh,
        in_specs=placed,
        out_specs=P(("row", "col"), "depth", None, None),
        check_vma=False,
    )
```

```python
import jax
import jax.numpy as jnp
from jax import lax
from jax.experimental import pallas as pl
from jax.experimental.pallas import tpu as pltpu
from jax.sharding import PartitionSpec as P

REACH = 8
WIDE = 2 * REACH
SPAN = 2 * REACH + 2


def permuted(value, axes, pairs):
    return lax.ppermute(value, axes, pairs)


together = lax.optimization_barrier


def line_window(own, extra):
    send_x = (lax.axis_index("col") == 0) == (lax.axis_index("row") % 2 == 0)

    def along_z(value):
        return permuted(value, "depth", [(0, 1), (1, 2), (2, 3), (3, 0)])

    def along_x(value):
        return permuted(value, "row", [(0, 1), (1, 0), (2, 3), (3, 2)])

    def along_y(value):
        return permuted(value, "row", [(0, 2), (2, 0), (1, 3), (3, 1)])

    def over_core(value):
        return permuted(value, "col", [(0, 1), (1, 0)])

    def shared(by_x, by_y):
        return over_core(jnp.where(send_x, by_x, by_y))

    def round_one(own):
        return together((own, along_x(own), along_z(own), over_core(own)))

    def round_two(own, x0, p1, c0):
        return own, c0, *together((x0, p1, along_x(p1), along_y(x0), along_z(p1)))

    def round_three(own, c0, x0, p1, x1, y0, p2):
        sent = along_x(p2), along_y(x1), along_z(p2), over_core(p1), shared(x0, y0)
        return own, c0, x0, p1, y0, *together((x1, p2, *sent))

    def round_four(own, c0, x0, p1, y0, x1, p2, x2, y1, p3, c1, s0):
        sent = along_x(p3), along_y(x2), over_core(p2), over_core(p3), shared(x1, y1)
        return own, c0, x0, p1, y0, x1, p2, y1, p3, c1, s0, *together((x2, *sent))

    def round_five(own, c0, x0, p1, y0, x1, p2, y1, p3, c1, s0, x2, x3, y2, c2, c3, s1):
        x3, y3, s2 = together((x3, along_y(x3), shared(x2, y2)))
        s3 = shared(x3, y3)
        pieces = own, p1, p2, p3
        return pieces, (c0, c1, c2, c3), (x0, x1, x2, x3), (y0, y1, y2, y3), (s0, s1, s2, s3)

    half = own.shape[0] // 2
    streams = [(own[:half],), (own[half:],)]
    for one_round in (round_one, round_two, round_three, round_four, round_five):
        streams = [one_round(*stream) for stream in streams]
        if one_round is round_one:
            extra, streams[1] = together((extra, streams[1]))
    groups = [[(a, b) for a, b in zip(*both)] for both in zip(*streams)]
    return groups, extra


def ring_window(own, extra):
    depths = lax.axis_size("depth")
    pieces = [own]
    for step in range(1, depths):
        pairs = [(i, (i + step) % depths) for i in range(depths)]
        pieces.append(permuted(own, "depth", pairs))
    count = lax.axis_size(("row", "col"))
    groups = [[(p,) for p in pieces]]
    for offset in (1, -1, 2, -2):
        pairs = [(i, (i - offset) % count) for i in range(count)]
        groups.append([(permuted(p, ("row", "col"), pairs),) for p in pieces])
    return groups, extra


def window_plan():
    sizes = (lax.axis_size("row"), lax.axis_size("col"), lax.axis_size("depth"))
    return line_window if sizes == (4, 2, 4) else ring_window


def purify_kernel(piece_count, piece_rows, piece_slots, own_rows, out_slots, *refs):
    place_ref, hole_ref, keep_ref, target_ref = refs[:4]
    piece_refs = refs[4 : 4 + piece_count]
    out_ref, panel, square, sem = refs[4 + piece_count :]
    window = own_rows + 2 * WIDE
    pairs = window // 2
    edge = out_ref.shape[-1]
    per_piece = piece_rows * piece_slots

    zero = jnp.zeros((edge, edge), jnp.bfloat16)

    for pair in range(pairs):
        base = pair * 2 * SPAN
        for half in range(2):
            for u in range(SPAN):
                row = 2 * pair - REACH + u
                inside = 0 <= row < window
                banded = (u < SPAN - 1) if half == 0 else (u > 0)
                if not (inside and banded):
                    panel[base + half * SPAN + u] = zero

    @pl.loop(0, window)
    def _(row):
        spot = hole_ref[row]

        @pl.when(spot >= 0)
        def _():
            panel[spot] = zero

    started = jnp.int32(0)
    for number, piece in enumerate(piece_refs):

        def start(row, done, number=number, piece=piece):
            for slot in range(piece_slots):
                spot = place_ref[number * per_piece + row * piece_slots + slot]

                @pl.when(spot >= 0)
                def _():
                    pltpu.make_async_copy(piece.at[row, slot], panel.at[spot], sem).start()

                done = done + jnp.where(spot >= 0, 1, 0)
            return done

        started = lax.fori_loop(0, piece_rows, start, started)

    @pl.loop(0, square.shape[0])
    def _(spot):
        square[spot] = zero

    @pl.loop(0, started)
    def _(_):
        pltpu.make_async_copy(piece_refs[0].at[0, 0], panel.at[0], sem).wait()

    cols = window + 2 * REACH
    first_pair = WIDE // 2

    @pl.loop(0, own_rows // 2)
    def _(pair_of_rows):
        base = (pair_of_rows + first_pair) * 2 * SPAN
        for delta in range(-REACH, REACH + 1):
            inner = range(max(delta, 0) - REACH // 2, min(delta, 0) + REACH // 2 + 1)
            left = jnp.concatenate(
                [
                    jnp.concatenate(
                        [
                            panel[base + e * 2 * SPAN + h * SPAN + a - 2 * e + REACH]
                            for e in inner
                            for h in range(2)
                        ],
                        axis=1,
                    )
                    for a in range(2)
                ],
                axis=0,
            )
            right = jnp.concatenate(
                [
                    panel[
                        pl.ds(
                            base + delta * 2 * SPAN + h * SPAN + 2 * (inner[0] - delta) + REACH,
                            2 * len(inner),
                        )
                    ].reshape(2 * len(inner) * edge, edge)
                    for h in range(2)
                ],
                axis=1,
            )
            both = jnp.dot(left, right, preferred_element_type=jnp.float32)
            for a in range(2):
                for h in range(2):
                    row = 2 * pair_of_rows + a
                    col = 2 * (pair_of_rows + first_pair + delta) + h
                    keep = keep_ref[row * window + col]
                    part = both[a * edge : (a + 1) * edge, h * edge : (h + 1) * edge]
                    part = jnp.where(keep > 0, part, 0.0)
                    square[row * cols + col + REACH] = part.astype(jnp.bfloat16)

    @pl.loop(0, own_rows)
    def _(row):
        for slot in range(out_slots):
            col = target_ref[row * out_slots + slot]
            pair = lax.shift_right_logical(col, 1)
            half = col - 2 * pair
            left = square[pl.ds(row * cols + 2 * pair, SPAN)]
            left = jnp.concatenate([left[u] for u in range(SPAN)], axis=1)
            right = panel[pl.ds((2 * pair + half) * SPAN, SPAN)].reshape(SPAN * edge, edge)
            cubed = jnp.dot(left, right, preferred_element_type=jnp.float32)
            own = square[row * cols + col + REACH].astype(jnp.float32)
            out_ref[row, slot] = (3.0 * own - 2.0 * cubed).astype(out_ref.dtype)


def window_places(place, depth):
    depths = lax.axis_size("depth")
    owners = [(depth - step) % depths for step in range(depths)]
    if window_plan() is not line_window:
        return owners, [0, 1, -1, 2, -2]
    beside = jnp.where(lax.axis_index("col") == 0, 1, -1)
    over = jnp.where(lax.axis_index("row") % 2 == 0, 2, -2)
    return owners, [0, beside, over, -over, -beside]


def local(blocks, block_cols, product_cols):
    rows, slots, edge = blocks.shape[0], blocks.shape[1], blocks.shape[2]
    order = block_cols.shape[0]
    targets = product_cols.shape[1]
    depth_count = lax.axis_size("depth")
    out_slots = targets // depth_count
    place = lax.axis_index(("row", "col"))
    depth = lax.axis_index("depth")
    window = rows + 2 * WIDE
    first = place * rows - WIDE

    owners, offsets = window_places(place, depth)
    row_ids = jnp.stack([(place + o) * rows + jnp.arange(rows) for o in offsets])
    slot_ids = jnp.stack([o * slots + jnp.arange(slots) for o in owners])
    wanted = block_cols[row_ids[:, None, :, None] % order, slot_ids[None, :, None, :]]

    def spot_of(row, col):
        pair = col // 2
        spot = (2 * pair + col % 2) * SPAN + row - 2 * pair + REACH
        return jnp.where(col < window, spot, -1).astype(jnp.int32)

    spots = spot_of(row_ids[:, None, :, None] - first, (wanted - first) % order).reshape(-1)
    all_rows = jnp.arange(window)
    filled = (block_cols[(all_rows + first) % order] - (all_rows + first)[:, None] + REACH) % order
    hole = (2 * REACH) * (2 * REACH + 1) // 2 - jnp.sum(filled, axis=1)
    hole_col = all_rows + hole - REACH
    holes = jnp.where(hole_col >= 0, spot_of(all_rows, hole_col), -1).astype(jnp.int32)
    target_cols = (product_cols - first) % order
    keep = jnp.any(target_cols[:, :, None] == jnp.arange(window), axis=1)
    keep = keep.astype(jnp.int32).reshape(-1)
    mine = lax.dynamic_slice_in_dim(target_cols, depth * out_slots, out_slots, 1)
    mine = mine.astype(jnp.int32).reshape(-1)

    groups, tables = window_plan()(blocks, (spots, holes, keep, mine))
    flat = [part for group in groups for piece in group for part in piece]
    kernel_body = lambda *refs: purify_kernel(
        len(flat), flat[0].shape[0], slots, rows, out_slots, *refs
    )
    smem = pl.BlockSpec(memory_space=pltpu.SMEM)
    hbm = pl.BlockSpec(memory_space=pl.ANY)
    return pl.pallas_call(
        kernel_body,
        out_shape=jax.ShapeDtypeStruct((rows, out_slots, edge, edge), jnp.bfloat16),
        in_specs=[smem] * 4 + [hbm] * len(flat),
        out_specs=pl.BlockSpec(memory_space=pltpu.VMEM),
        scratch_shapes=[
            pltpu.VMEM((window * SPAN, edge, edge), jnp.bfloat16),
            pltpu.VMEM((rows * (window + 2 * REACH), edge, edge), jnp.bfloat16),
            pltpu.SemaphoreType.DMA,
        ],
        compiler_params=pltpu.CompilerParams(vmem_limit_bytes=56 * 2**20),
        name="purify",
    )(*tables, *flat)


def solution(mesh):
    placed = (P(("row", "col"), "depth", None, None), P(), P(("row", "col"), None))
    return jax.shard_map(
        local,
        mesh=mesh,
        in_specs=placed,
        out_specs=P(("row", "col"), "depth", None, None),
        check_vma=False,
    )
```

```python
import jax
import jax.numpy as jnp
from jax import lax
from jax.experimental import pallas as pl
from jax.experimental.pallas import tpu as pltpu
from jax.sharding import PartitionSpec as P

REACH = 8
WIDE = 2 * REACH
SPAN = 2 * REACH + 2


def permuted(value, axes, pairs):
    return lax.ppermute(value, axes, pairs)


together = lax.optimization_barrier


def line_window(own, extra):
    send_x = (lax.axis_index("col") == 0) == (lax.axis_index("row") % 2 == 0)

    def along_z(value):
        return permuted(value, "depth", [(0, 1), (1, 2), (2, 3), (3, 0)])

    def along_x(value):
        return permuted(value, "row", [(0, 1), (1, 0), (2, 3), (3, 2)])

    def along_y(value):
        return permuted(value, "row", [(0, 2), (2, 0), (1, 3), (3, 1)])

    def over_core(value):
        return permuted(value, "col", [(0, 1), (1, 0)])

    def shared(by_x, by_y):
        return over_core(jnp.where(send_x, by_x, by_y))

    def round_one(own):
        return together((own, along_x(own), along_z(own)))

    def round_two(own, x0, p1):
        return own, *together((x0, p1, along_x(p1), along_y(x0), along_z(p1)))

    def round_three(own, x0, p1, x1, y0, p2):
        sent = along_x(p2), along_y(x1), along_z(p2), shared(x0, y0)
        return own, x0, p1, y0, *together((x1, p2, *sent))

    def round_four(own, x0, p1, y0, x1, p2, x2, y1, p3, s0):
        sent = along_x(p3), along_y(x2), shared(x1, y1), over_core(p1)
        return own, x0, p1, y0, x1, y1, s0, *together((p2, p3, x2, *sent))

    def round_five(own, x0, p1, y0, x1, y1, s0, p2, p3, x2, x3, y2, s1, c1):
        sent = along_y(x3), shared(x2, y2), over_core(p2), over_core(p3)
        x3, y3, s2, c2, c3 = together((x3, *sent))
        x, y, s = (x0, x1, x2, x3), (y0, y1, y2, y3), (s0, s1, s2, shared(x3, y3))
        return (own, p1, p2, p3), (c1, c2, c3), x, y, s

    half = own.shape[0] // 2
    streams = [round_one(own[:half]), round_one(own[half:])]
    extra, streams[1] = together((extra, streams[1]))
    for one_round in (round_two, round_three):
        streams = [one_round(*stream) for stream in streams]
    own, streams[0] = together((own, streams[0]))
    c0 = over_core(own)
    streams = [round_four(*stream) for stream in streams]
    c0, streams[1] = together((c0, streams[1]))
    groups = [list(zip(*parts)) for parts in zip(*[round_five(*one) for one in streams])]
    groups[1].insert(0, (c0,))
    return groups, extra


def ring_window(own, extra):
    depths = lax.axis_size("depth")
    pieces = [own]
    for step in range(1, depths):
        pairs = [(i, (i + step) % depths) for i in range(depths)]
        pieces.append(permuted(own, "depth", pairs))
    count = lax.axis_size(("row", "col"))
    groups = [[(p,) for p in pieces]]
    for offset in (1, -1, 2, -2):
        pairs = [(i, (i - offset) % count) for i in range(count)]
        groups.append([(permuted(p, ("row", "col"), pairs),) for p in pieces])
    return groups, extra


def window_plan():
    sizes = (lax.axis_size("row"), lax.axis_size("col"), lax.axis_size("depth"))
    return line_window if sizes == (4, 2, 4) else ring_window


def purify_kernel(piece_count, own_rows, out_slots, *refs):
    place_ref, hole_ref, keep_ref, target_ref = refs[:4]
    piece_refs = refs[4 : 4 + piece_count]
    out_ref, panel, square, sem = refs[4 + piece_count :]
    window = own_rows + 2 * WIDE
    pairs = window // 2
    edge = out_ref.shape[-1]

    zero = jnp.zeros((edge, edge), jnp.bfloat16)

    for pair in range(pairs):
        base = pair * 2 * SPAN
        for half in range(2):
            for u in range(SPAN):
                row = 2 * pair - REACH + u
                inside = 0 <= row < window
                banded = (u < SPAN - 1) if half == 0 else (u > 0)
                if not (inside and banded):
                    panel[base + half * SPAN + u] = zero

    @pl.loop(0, window)
    def _(row):
        spot = hole_ref[row]

        @pl.when(spot >= 0)
        def _():
            panel[spot] = zero

    started = jnp.int32(0)
    first = 0
    for piece in piece_refs:
        piece_rows, piece_slots = piece.shape[:2]

        def start(row, done, first=first, piece=piece, piece_slots=piece_slots):
            for slot in range(piece_slots):
                spot = place_ref[first + row * piece_slots + slot]

                @pl.when(spot >= 0)
                def _():
                    pltpu.make_async_copy(piece.at[row, slot], panel.at[spot], sem).start()

                done = done + jnp.where(spot >= 0, 1, 0)
            return done

        started = lax.fori_loop(0, piece_rows, start, started)
        first += piece_rows * piece_slots

    @pl.loop(0, square.shape[0])
    def _(spot):
        square[spot] = zero

    @pl.loop(0, started)
    def _(_):
        pltpu.make_async_copy(piece_refs[0].at[0, 0], panel.at[0], sem).wait()

    cols = window + 2 * REACH
    first_pair = WIDE // 2

    @pl.loop(0, own_rows // 2)
    def _(pair_of_rows):
        base = (pair_of_rows + first_pair) * 2 * SPAN
        for delta in range(-REACH, REACH + 1):
            inner = range(max(delta, 0) - REACH // 2, min(delta, 0) + REACH // 2 + 1)
            left = jnp.concatenate(
                [
                    jnp.concatenate(
                        [
                            panel[base + e * 2 * SPAN + h * SPAN + a - 2 * e + REACH]
                            for e in inner
                            for h in range(2)
                        ],
                        axis=1,
                    )
                    for a in range(2)
                ],
                axis=0,
            )
            right = jnp.concatenate(
                [
                    panel[
                        pl.ds(
                            base + delta * 2 * SPAN + h * SPAN + 2 * (inner[0] - delta) + REACH,
                            2 * len(inner),
                        )
                    ].reshape(2 * len(inner) * edge, edge)
                    for h in range(2)
                ],
                axis=1,
            )
            both = jnp.dot(left, right, preferred_element_type=jnp.float32)
            for a in range(2):
                for h in range(2):
                    row = 2 * pair_of_rows + a
                    col = 2 * (pair_of_rows + first_pair + delta) + h
                    keep = keep_ref[row * window + col]
                    part = both[a * edge : (a + 1) * edge, h * edge : (h + 1) * edge]
                    part = jnp.where(keep > 0, part, 0.0)
                    square[row * cols + col + REACH] = part.astype(jnp.bfloat16)

    @pl.loop(0, own_rows)
    def _(row):
        for slot in range(out_slots):
            col = target_ref[row * out_slots + slot]
            pair = lax.shift_right_logical(col, 1)
            half = col - 2 * pair
            left = square[pl.ds(row * cols + 2 * pair, SPAN)]
            left = jnp.concatenate([left[u] for u in range(SPAN)], axis=1)
            right = panel[pl.ds((2 * pair + half) * SPAN, SPAN)].reshape(SPAN * edge, edge)
            cubed = jnp.dot(left, right, preferred_element_type=jnp.float32)
            own = square[row * cols + col + REACH].astype(jnp.float32)
            out_ref[row, slot] = (3.0 * own - 2.0 * cubed).astype(out_ref.dtype)


def window_places(place, depth):
    depths = lax.axis_size("depth")
    owners = [(depth - step) % depths for step in range(depths)]
    if window_plan() is not line_window:
        return owners, [0, 1, -1, 2, -2]
    beside = jnp.where(lax.axis_index("col") == 0, 1, -1)
    over = jnp.where(lax.axis_index("row") % 2 == 0, 2, -2)
    return owners, [0, beside, over, -over, -beside]


def local(blocks, block_cols, product_cols):
    rows, slots, edge = blocks.shape[0], blocks.shape[1], blocks.shape[2]
    order = block_cols.shape[0]
    targets = product_cols.shape[1]
    depth_count = lax.axis_size("depth")
    out_slots = targets // depth_count
    place = lax.axis_index(("row", "col"))
    depth = lax.axis_index("depth")
    window = rows + 2 * WIDE
    first = place * rows - WIDE

    owners, offsets = window_places(place, depth)
    row_ids = jnp.stack([(place + o) * rows + jnp.arange(rows) for o in offsets])
    slot_ids = jnp.stack([o * slots + jnp.arange(slots) for o in owners])
    wanted = block_cols[row_ids[:, None, :, None] % order, slot_ids[None, :, None, :]]

    def spot_of(row, col):
        pair = col // 2
        spot = (2 * pair + col % 2) * SPAN + row - 2 * pair + REACH
        return jnp.where(col < window, spot, -1).astype(jnp.int32)

    spots = spot_of(row_ids[:, None, :, None] - first, (wanted - first) % order).reshape(-1)
    all_rows = jnp.arange(window)
    filled = (block_cols[(all_rows + first) % order] - (all_rows + first)[:, None] + REACH) % order
    hole = (2 * REACH) * (2 * REACH + 1) // 2 - jnp.sum(filled, axis=1)
    hole_col = all_rows + hole - REACH
    holes = jnp.where(hole_col >= 0, spot_of(all_rows, hole_col), -1).astype(jnp.int32)
    target_cols = (product_cols - first) % order
    keep = jnp.any(target_cols[:, :, None] == jnp.arange(window), axis=1)
    keep = keep.astype(jnp.int32).reshape(-1)
    mine = lax.dynamic_slice_in_dim(target_cols, depth * out_slots, out_slots, 1)
    mine = mine.astype(jnp.int32).reshape(-1)

    groups, tables = window_plan()(blocks, (spots, holes, keep, mine))
    flat = [part for group in groups for piece in group for part in piece]
    kernel_body = lambda *refs: purify_kernel(len(flat), rows, out_slots, *refs)
    smem = pl.BlockSpec(memory_space=pltpu.SMEM)
    hbm = pl.BlockSpec(memory_space=pl.ANY)
    return pl.pallas_call(
        kernel_body,
        out_shape=jax.ShapeDtypeStruct((rows, out_slots, edge, edge), jnp.bfloat16),
        in_specs=[smem] * 4 + [hbm] * len(flat),
        out_specs=pl.BlockSpec(memory_space=pltpu.VMEM),
        scratch_shapes=[
            pltpu.VMEM((window * SPAN, edge, edge), jnp.bfloat16),
            pltpu.VMEM((rows * (window + 2 * REACH), edge, edge), jnp.bfloat16),
            pltpu.SemaphoreType.DMA,
        ],
        compiler_params=pltpu.CompilerParams(vmem_limit_bytes=56 * 2**20),
        name="purify",
    )(*tables, *flat)


def solution(mesh):
    placed = (P(("row", "col"), "depth", None, None), P(), P(("row", "col"), None))
    return jax.shard_map(
        local,
        mesh=mesh,
        in_specs=placed,
        out_specs=P(("row", "col"), "depth", None, None),
        check_vma=False,
    )
```

```python
import jax
import jax.numpy as jnp
from jax import lax
from jax.experimental import pallas as pl
from jax.experimental.pallas import tpu as pltpu
from jax.sharding import PartitionSpec as P

REACH = 8
WIDE = 2 * REACH
SPAN = 2 * REACH + 2


def permuted(value, axes, pairs):
    return lax.ppermute(value, axes, pairs)


together = lax.optimization_barrier


def line_window(own, extra):
    send_x = (lax.axis_index("col") == 0) == (lax.axis_index("row") % 2 == 0)

    def along_z(value):
        return permuted(value, "depth", [(0, 1), (1, 2), (2, 3), (3, 0)])

    def along_x(value):
        return permuted(value, "row", [(0, 1), (1, 0), (2, 3), (3, 2)])

    def along_y(value):
        return permuted(value, "row", [(0, 2), (2, 0), (1, 3), (3, 1)])

    def over_core(value):
        return permuted(value, "col", [(0, 1), (1, 0)])

    def shared(by_x, by_y):
        return over_core(jnp.where(send_x, by_x, by_y))

    def round_one(own):
        return together((own, along_x(own), along_z(own)))

    def round_two(own, x0, p1):
        return own, *together((x0, p1, along_x(p1), along_y(x0), along_z(p1)))

    def round_three(own, x0, p1, x1, y0, p2):
        sent = along_x(p2), along_y(x1), along_z(p2), shared(x0, y0)
        return own, x0, p1, y0, *together((x1, p2, *sent))

    def round_four(own, x0, p1, y0, x1, p2, x2, y1, p3, s0):
        sent = along_x(p3), along_y(x2), shared(x1, y1), over_core(p1)
        return own, x0, p1, y0, x1, y1, s0, *together((p2, p3, x2, *sent))

    half = own.shape[0] // 2
    streams = [round_one(own[:half]), round_one(own[half:])]
    extra, streams[1] = together((extra, streams[1]))
    for one_round in (round_two, round_three):
        streams = [one_round(*stream) for stream in streams]
    own, streams[0] = together((own, streams[0]))
    c0 = over_core(own)
    streams = [round_four(*stream) for stream in streams]
    c0, streams[1] = together((c0, streams[1]))
    p0, x0, p1, y0, x1, y1, s0, p2, p3, x2, x3, y2, s1, c1 = map(list, zip(*streams))

    def to_other(h):
        return shared(x2[h], y2[h]), over_core(p2[h]), over_core(p3[h])

    first = along_y(x3[0])
    x3[1], x2[0], y2[0], p2[0], p3[0] = together((x3[1], x2[0], y2[0], p2[0], p3[0]))
    second = along_y(x3[1])
    crossed = to_other(0)
    first, crossed, x2[1], y2[1], p2[1], p3[1] = together(
        (first, crossed, x2[1], y2[1], p2[1], p3[1])
    )
    s3 = shared(x3[0], first)
    second, s3, after = together((second, s3, to_other(1)))
    s3 = s3, shared(x3[1], second)
    s2, c2, c3 = zip(crossed, after)
    groups = [
        [p0, p1, p2, p3],
        [(c0,), c1, c2, c3],
        [x0, x1, x2, x3],
        [y0, y1, y2, (first, second)],
        [s0, s1, s2, s3],
    ]
    return groups, extra


def ring_window(own, extra):
    depths = lax.axis_size("depth")
    pieces = [own]
    for step in range(1, depths):
        pairs = [(i, (i + step) % depths) for i in range(depths)]
        pieces.append(permuted(own, "depth", pairs))
    count = lax.axis_size(("row", "col"))
    groups = [[(p,) for p in pieces]]
    for offset in (1, -1, 2, -2):
        pairs = [(i, (i - offset) % count) for i in range(count)]
        groups.append([(permuted(p, ("row", "col"), pairs),) for p in pieces])
    return groups, extra


def window_plan():
    sizes = (lax.axis_size("row"), lax.axis_size("col"), lax.axis_size("depth"))
    return line_window if sizes == (4, 2, 4) else ring_window


def purify_kernel(piece_count, own_rows, out_slots, *refs):
    place_ref, hole_ref, keep_ref, target_ref = refs[:4]
    piece_refs = refs[4 : 4 + piece_count]
    out_ref, panel, square, sem = refs[4 + piece_count :]
    window = own_rows + 2 * WIDE
    pairs = window // 2
    edge = out_ref.shape[-1]

    zero = jnp.zeros((edge, edge), jnp.bfloat16)

    for pair in range(pairs):
        base = pair * 2 * SPAN
        for half in range(2):
            for u in range(SPAN):
                row = 2 * pair - REACH + u
                inside = 0 <= row < window
                banded = (u < SPAN - 1) if half == 0 else (u > 0)
                if not (inside and banded):
                    panel[base + half * SPAN + u] = zero

    @pl.loop(0, window)
    def _(row):
        spot = hole_ref[row]

        @pl.when(spot >= 0)
        def _():
            panel[spot] = zero

    started = jnp.int32(0)
    first = 0
    for piece in piece_refs:
        piece_rows, piece_slots = piece.shape[:2]

        def start(row, done, first=first, piece=piece, piece_slots=piece_slots):
            for slot in range(piece_slots):
                spot = place_ref[first + row * piece_slots + slot]

                @pl.when(spot >= 0)
                def _():
                    pltpu.make_async_copy(piece.at[row, slot], panel.at[spot], sem).start()

                done = done + jnp.where(spot >= 0, 1, 0)
            return done

        started = lax.fori_loop(0, piece_rows, start, started)
        first += piece_rows * piece_slots

    @pl.loop(0, square.shape[0])
    def _(spot):
        square[spot] = zero

    @pl.loop(0, started)
    def _(_):
        pltpu.make_async_copy(piece_refs[0].at[0, 0], panel.at[0], sem).wait()

    cols = window + 2 * REACH
    first_pair = WIDE // 2

    @pl.loop(0, own_rows // 2)
    def _(pair_of_rows):
        base = (pair_of_rows + first_pair) * 2 * SPAN
        for delta in range(-REACH, REACH + 1):
            inner = range(max(delta, 0) - REACH // 2, min(delta, 0) + REACH // 2 + 1)
            left = jnp.concatenate(
                [
                    jnp.concatenate(
                        [
                            panel[base + e * 2 * SPAN + h * SPAN + a - 2 * e + REACH]
                            for e in inner
                            for h in range(2)
                        ],
                        axis=1,
                    )
                    for a in range(2)
                ],
                axis=0,
            )
            right = jnp.concatenate(
                [
                    panel[
                        pl.ds(
                            base + delta * 2 * SPAN + h * SPAN + 2 * (inner[0] - delta) + REACH,
                            2 * len(inner),
                        )
                    ].reshape(2 * len(inner) * edge, edge)
                    for h in range(2)
                ],
                axis=1,
            )
            both = jnp.dot(left, right, preferred_element_type=jnp.float32)
            for a in range(2):
                for h in range(2):
                    row = 2 * pair_of_rows + a
                    col = 2 * (pair_of_rows + first_pair + delta) + h
                    keep = keep_ref[row * window + col]
                    part = both[a * edge : (a + 1) * edge, h * edge : (h + 1) * edge]
                    part = jnp.where(keep > 0, part, 0.0)
                    square[row * cols + col + REACH] = part.astype(jnp.bfloat16)

    @pl.loop(0, own_rows)
    def _(row):
        for slot in range(out_slots):
            col = target_ref[row * out_slots + slot]
            pair = lax.shift_right_logical(col, 1)
            half = col - 2 * pair
            left = square[pl.ds(row * cols + 2 * pair, SPAN)]
            left = jnp.concatenate([left[u] for u in range(SPAN)], axis=1)
            right = panel[pl.ds((2 * pair + half) * SPAN, SPAN)].reshape(SPAN * edge, edge)
            cubed = jnp.dot(left, right, preferred_element_type=jnp.float32)
            own = square[row * cols + col + REACH].astype(jnp.float32)
            out_ref[row, slot] = (3.0 * own - 2.0 * cubed).astype(out_ref.dtype)


def window_places(place, depth):
    depths = lax.axis_size("depth")
    owners = [(depth - step) % depths for step in range(depths)]
    if window_plan() is not line_window:
        return owners, [0, 1, -1, 2, -2]
    beside = jnp.where(lax.axis_index("col") == 0, 1, -1)
    over = jnp.where(lax.axis_index("row") % 2 == 0, 2, -2)
    return owners, [0, beside, over, -over, -beside]


def local(blocks, block_cols, product_cols):
    rows, slots, edge = blocks.shape[0], blocks.shape[1], blocks.shape[2]
    order = block_cols.shape[0]
    targets = product_cols.shape[1]
    depth_count = lax.axis_size("depth")
    out_slots = targets // depth_count
    place = lax.axis_index(("row", "col"))
    depth = lax.axis_index("depth")
    window = rows + 2 * WIDE
    first = place * rows - WIDE

    owners, offsets = window_places(place, depth)
    row_ids = jnp.stack([(place + o) * rows + jnp.arange(rows) for o in offsets])
    slot_ids = jnp.stack([o * slots + jnp.arange(slots) for o in owners])
    wanted = block_cols[row_ids[:, None, :, None] % order, slot_ids[None, :, None, :]]

    def spot_of(row, col):
        pair = col // 2
        spot = (2 * pair + col % 2) * SPAN + row - 2 * pair + REACH
        return jnp.where(col < window, spot, -1).astype(jnp.int32)

    spots = spot_of(row_ids[:, None, :, None] - first, (wanted - first) % order).reshape(-1)
    all_rows = jnp.arange(window)
    filled = (block_cols[(all_rows + first) % order] - (all_rows + first)[:, None] + REACH) % order
    hole = (2 * REACH) * (2 * REACH + 1) // 2 - jnp.sum(filled, axis=1)
    hole_col = all_rows + hole - REACH
    holes = jnp.where(hole_col >= 0, spot_of(all_rows, hole_col), -1).astype(jnp.int32)
    target_cols = (product_cols - first) % order
    keep = jnp.any(target_cols[:, :, None] == jnp.arange(window), axis=1)
    keep = keep.astype(jnp.int32).reshape(-1)
    mine = lax.dynamic_slice_in_dim(target_cols, depth * out_slots, out_slots, 1)
    mine = mine.astype(jnp.int32).reshape(-1)

    groups, tables = window_plan()(blocks, (spots, holes, keep, mine))
    flat = [part for group in groups for piece in group for part in piece]
    kernel_body = lambda *refs: purify_kernel(len(flat), rows, out_slots, *refs)
    smem = pl.BlockSpec(memory_space=pltpu.SMEM)
    hbm = pl.BlockSpec(memory_space=pl.ANY)
    return pl.pallas_call(
        kernel_body,
        out_shape=jax.ShapeDtypeStruct((rows, out_slots, edge, edge), jnp.bfloat16),
        in_specs=[smem] * 4 + [hbm] * len(flat),
        out_specs=pl.BlockSpec(memory_space=pltpu.VMEM),
        scratch_shapes=[
            pltpu.VMEM((window * SPAN, edge, edge), jnp.bfloat16),
            pltpu.VMEM((rows * (window + 2 * REACH), edge, edge), jnp.bfloat16),
            pltpu.SemaphoreType.DMA,
        ],
        compiler_params=pltpu.CompilerParams(vmem_limit_bytes=56 * 2**20),
        name="purify",
    )(*tables, *flat)


def solution(mesh):
    placed = (P(("row", "col"), "depth", None, None), P(), P(("row", "col"), None))
    return jax.shard_map(
        local,
        mesh=mesh,
        in_specs=placed,
        out_specs=P(("row", "col"), "depth", None, None),
        check_vma=False,
    )
```
